1024 devices in a mesh: loss: 64 (over z_lo, x), section: 4 (over y), mp: 4 (over z_hi, core).
Axes of the slice: x: 4, y: 4, z: 32 (z_hi: 2, z_lo: 16; z = z_hi * 16 + z_lo), core: 2. Of those that a mesh axis runs over, the one named last changes fastest.
Arguments:
- image_embed: bfloat16 [16384, 1152], P('loss'), may hold values from -0.1796875 to 0.1796875
- text_embed: bfloat16 [16384, 1152], P(('loss', 'section', 'mp')), may hold values from -0.1796875 to 0.1796875
- logit_scale: float32 [], replicated, may hold values from 4 to 16
- logit_bias: float32 [], replicated, may hold values from -3 to -1
Outputs:
- grad_image: float32 [16384, 1152], P(('loss', 'section', 'mp'))
- grad_text: float32 [16384, 1152], P(('loss', 'section', 'mp'))
The draws below stay inside these ranges and needn't reach their ends.
All inputs are finite; a program needn't handle non-finite values.
Results may differ from the reference program's by a relative error of at most 0.017.
Values may be sent and summed in bfloat16 or wider, within the bound.
A program may use at most 32 MiB of HBM per device.

```python
import math
import jax
import jax.numpy as jnp
from jax import lax

E = 1152
PAIRS = 16384
N_LOSS = 64


def level_of(key, shape, pieces, low, top_value):
    factor_of = 1.0
    for axis_at, blocks in pieces:
        heights = jax.random.uniform(jax.random.fold_in(jax.random.fold_in(key, 6), axis_at), (blocks,), jnp.float32, low / len(pieces), top_value / len(pieces))
        factor_of = factor_of * jnp.repeat(jnp.exp(heights), shape[axis_at] // blocks).reshape((-1,) + (1,) * (len(shape) - 1 - axis_at))
    return factor_of


def normal_values(rng, shape, spread, reach, cuts=(), held_as=jnp.bfloat16):
    drawn = spread * jax.random.normal(rng, shape, jnp.float32)
    if cuts:
        drawn = drawn * level_of(rng, shape, cuts, -0.22, 0.18)
    return jnp.clip(drawn, -reach, reach).astype(held_as)


def setup_inputs(seed: int = 0) -> dict:
    keys = jax.random.split(jax.random.key(seed), 5)
    return {
        "image_embed": normal_values(keys[0], (PAIRS, E), 0.03, 0.1796875, ((0, 64),)),
        "text_embed": normal_values(keys[1], (PAIRS, E), 0.03, 0.1796875, ((0, 1024),)),
        "logit_scale": jnp.clip(jnp.exp(jax.random.uniform(keys[2], (), jnp.float32, math.log(4.0), math.log(16.0))), 4.0, 16.0),
        "logit_bias": jnp.clip(jax.random.uniform(keys[3], (), jnp.float32, -3.0, -1.0), -3.0, -1.0),
    }


epsilon = 1e-06

def unit_rows(values):
    widened = values.astype(jnp.float32)
    scaling = lax.rsqrt(lax.optimization_barrier(jnp.sum(widened * widened, axis=-1, keepdims=True)) + epsilon)
    return (widened * scaling, scaling)

def unit_backward(unit, scaling, gradient):
    return (gradient - unit * lax.optimization_barrier(jnp.sum(unit * gradient, axis=-1, keepdims=True))) * scaling

def reference(image_embed, text_embed, logit_scale, logit_bias):
    unit_image, image_scaling = unit_rows(image_embed)
    unit_text, text_scaling = unit_rows(text_embed)
    image_low = unit_image.astype(jnp.bfloat16)
    text_low = unit_text.astype(jnp.bfloat16)
    pair_count = image_low.shape[0]
    width = image_low.shape[1]
    block_rows = pair_count // N_LOSS
    image_blocks = image_low.reshape(N_LOSS, block_rows, width)
    columns = jnp.arange(pair_count, dtype=jnp.int32)

    def visit(text_grad, scan_item):
        block_index, image_block = scan_item
        logits = logit_scale * jnp.dot(image_block, text_low.T, preferred_element_type=jnp.float32) + logit_bias
        row_ids = block_index * block_rows + jnp.arange(block_rows, dtype=jnp.int32)
        positive = (row_ids[:, None] == columns[None, :]).astype(jnp.float32)
        dlogit = (jax.nn.sigmoid(logits) - positive).astype(jnp.bfloat16)
        image_grad = logit_scale * jnp.dot(dlogit, text_low, preferred_element_type=jnp.float32)
        text_grad = text_grad + logit_scale * jnp.dot(dlogit.T, image_block, preferred_element_type=jnp.float32)
        return (text_grad, image_grad)
    start = jnp.zeros((pair_count, width), jnp.float32)
    text_grad, image_grads = lax.scan(visit, start, (jnp.arange(N_LOSS, dtype=jnp.int32), image_blocks))
    image_grad = image_grads.reshape(pair_count, width)
    grad_image = unit_backward(unit_image, image_scaling, image_grad)
    grad_text = unit_backward(unit_text, text_scaling, text_grad)
    return (grad_image, grad_text)
```

```python
import functools

import jax
import jax.numpy as jnp
from jax import lax
from jax.experimental import pallas as pl
from jax.experimental.pallas import tpu as pltpu
from jax.sharding import PartitionSpec as P

epsilon = 1e-06
MESH = pl.DeviceIdType.MESH
F32 = jnp.float32
BF16 = jnp.bfloat16

RING = 4
HALVES = 2
CORES = 2


def unit_rows(values):
    widened = values.astype(F32)
    scaling = lax.rsqrt(jnp.sum(widened * widened, axis=-1, keepdims=True) + epsilon)
    return (widened * scaling, scaling)


def unit_backward(unit, scaling, gradient):
    return (gradient - unit * jnp.sum(unit * gradient, axis=-1, keepdims=True)) * scaling


class Plan:
    def __init__(self, send_sems, recv_sems):
        self.send_sems = send_sems
        self.recv_sems = recv_sems
        self.numbers = {}
        self.sends = []

    def number(self, key):
        return self.numbers.setdefault(key, len(self.numbers))

    def copy(self, key, source, target, device):
        at = self.number(key)
        return pltpu.make_async_remote_copy(
            src_ref=source,
            dst_ref=target,
            send_sem=self.send_sems.at[at],
            recv_sem=self.recv_sems.at[at],
            device_id=device,
            device_id_type=MESH,
        )

    def send(self, key, source, target, device):
        copy = self.copy(key, source, target, device)
        copy.start()
        self.sends.append(copy)

    def arrive(self, key, target, device):
        self.copy(key, target, target, device).wait_recv()

    def finish(self):
        for copy in self.sends:
            copy.wait_send()


MOST_COPIES = 96


def kernel(
    zlo_size,
    scale_ref,
    bias_ref,
    image_ref,
    text_ref,
    grad_image_ref,
    grad_text_ref,
    images,
    texts,
    dlogits,
    partial,
    up_out,
    up_in,
    down_out,
    down_in,
    core_out,
    core_in,
    held,
    outer_out,
    first_next,
    first_prev,
    last_next,
    last_prev,
    inner_sum,
    inner_out,
    inner_first,
    inner_next,
    inner_prev,
    half_sum,
    half_out,
    half_in,
    send_sems,
    recv_sems,
):
    rows = text_ref.shape[0]
    width = text_ref.shape[1]
    blocks = zlo_size
    ups = blocks // 2
    downs = blocks - 1 - ups
    group = RING * RING * rows
    z_size = zlo_size * HALVES

    loss = lax.axis_index("loss")
    y = lax.axis_index("section")
    mp = lax.axis_index("mp")
    z_lo = lax.div(loss, RING)
    x = lax.rem(loss, RING)
    z_half = lax.div(mp, CORES)
    core = lax.rem(mp, CORES)
    z = z_half * zlo_size + z_lo

    def device(x_at, y_at, z_at, core_at):
        return {
            "loss": lax.rem(z_at, zlo_size) * RING + x_at,
            "section": y_at,
            "mp": lax.div(z_at, zlo_size) * CORES + core_at,
        }

    def ring(at, steps):
        return lax.rem(at + (steps + RING), RING)

    z_up = device(x, y, lax.rem(z + 1, z_size), core)
    z_down = device(x, y, lax.rem(z + (z_size - 1), z_size), core)
    z_far = device(x, y, lax.rem(z + zlo_size, z_size), core)
    x_next = device(ring(x, 1), y, z, core)
    x_prev = device(ring(x, -1), y, z, core)
    y_next = device(x, ring(y, 1), z, core)
    y_prev = device(x, ring(y, -1), z, core)
    other_core = 1 - core
    sibling = device(x, y, z, other_core)
    neighbours = (z_up, z_down, z_far, x_next, x_prev, y_next, y_prev, sibling)

    barrier = pltpu.get_barrier_semaphore()
    for neighbour in neighbours:
        pl.semaphore_signal(barrier, inc=1, device_id=neighbour, device_id_type=MESH)

    plan = Plan(send_sems, recv_sems)
    unit_text, text_scaling = unit_rows(text_ref[...])
    texts[0] = unit_text.astype(BF16)

    pl.semaphore_wait(barrier, len(neighbours))

    def slot_up(hop):
        return 0 if hop == 0 else 2 * hop - 1

    def slot_down(hop):
        return 2 * hop

    def text_up(hop):
        plan.send(("tu", hop), texts.at[slot_up(hop - 1)], texts.at[slot_up(hop)], z_up)

    def text_down(hop):
        plan.send(("td", hop), texts.at[slot_down(hop - 1)], texts.at[slot_down(hop)], z_down)

    def text_hop(hop):
        plan.arrive(("tu", hop), texts.at[slot_up(hop)], z_up)
        if hop < ups:
            text_up(hop + 1)
        if hop <= downs:
            plan.arrive(("td", hop), texts.at[slot_down(hop)], z_down)
            if hop < downs:
                text_down(hop + 1)

    text_up(1)
    if downs >= 1:
        text_down(1)

    for y_at in range(RING):
        for half_at in range(HALVES):
            for core_at in range(CORES):
                start = ((y_at * HALVES + half_at) * CORES + core_at) * rows
                low = unit_rows(image_ref[start : start + rows, :])[0].astype(BF16)
                if half_at == 0:
                    images[core_at, 0, x, y_at] = low
                else:
                    images[core_at, 1, y_at, x] = low

    def piece(half_at, core_at, x_at):
        if half_at == 0:
            return images.at[core_at, 0, x_at]
        return images.at[core_at, 1, :, x_at]

    for half_at in range(HALVES):
        own = piece(half_at, core, x)
        plan.send(("xn", half_at), own, own, x_next)
        plan.send(("xp", half_at), own, own, x_prev)

    def to_sibling(half_at, steps):
        mine = piece(half_at, core, ring(x, steps))
        plan.send(("xc", half_at, steps), mine, mine, sibling)

    def image_near(half_at):
        from_prev = piece(half_at, core, ring(x, -1))
        from_next = piece(half_at, core, ring(x, 1))
        plan.arrive(("xn", half_at), from_prev, x_next)
        if half_at == 0:
            plan.send(("xf", 0), from_prev, from_prev, x_next)
        plan.arrive(("xp", half_at), from_next, x_prev)
        if half_at == 1:
            plan.send(("xf", 1), from_next, from_next, x_prev)
        to_sibling(half_at, -1)
        to_sibling(half_at, 1)

    def image_far(half_at):
        plan.arrive(("xf", half_at), piece(half_at, core, ring(x, 2)), x_next)
        to_sibling(half_at, 2)

    def image_rest():
        for half_at in range(HALVES):
            for steps in (-1, 1, 2):
                theirs = piece(half_at, other_core, ring(x, steps))
                plan.arrive(("xc", half_at, steps), theirs, sibling)

    scale = scale_ref[0, 0]
    bias = bias_ref[0, 0]
    image_count = CORES * HALVES * group
    own_inner = jnp.where(z_half == 0, x * RING + y, y * RING + x)
    own_start = (core * HALVES + z_half) * group + own_inner * rows

    def batch(first, last):
        count = (last - first) * rows
        block = texts[first:last].reshape(count, width)
        every = images[...].reshape(image_count, width)
        logits = scale * lax.dot_general(
            block, every, (((1,), (1,)), ((), ())), preferred_element_type=F32
        )
        slope = jax.nn.sigmoid(logits + bias)
        if first == 0:
            text_ids = lax.broadcasted_iota(jnp.int32, (count, image_count), 0)
            image_ids = lax.broadcasted_iota(jnp.int32, (count, image_count), 1)
            positive = (text_ids < rows) & (image_ids == text_ids + own_start)
            slope = slope - jnp.where(positive, 1.0, 0.0)
        low = slope.astype(BF16)
        for core_at in range(CORES):
            for half_at in range(HALVES):
                start = (core_at * HALVES + half_at) * group
                dlogits[core_at, half_at, first * rows : last * rows, :] = low[:, start : start + group]
        grads = jnp.dot(low, every, preferred_element_type=F32)
        partial[first:last] = grads.reshape(last - first, rows, width)

    far_at = min(5, ups)
    cuts = {}
    if ups >= 8:
        cuts = {ups - 2: (0, 2 * (ups - 4) + 1), ups - 1: (2 * (ups - 4) + 1, 2 * (ups - 2) + 1), ups: (2 * (ups - 2) + 1, blocks)}
    else:
        cuts = {ups: (0, blocks)}
    images_ready = False
    for hop in range(1, ups + 1):
        text_hop(hop)
        if hop == min(2, ups):
            image_near(0)
        if hop == min(3, ups):
            image_near(1)
        if hop == far_at:
            image_far(0)
            image_far(1)
        if hop in cuts:
            if not images_ready:
                image_rest()
                images_ready = True
            batch(*cuts[hop])

    def back_down(step):
        slot = slot_up(ups + 1 - step)
        total = partial[slot]
        if step > 1:
            plan.arrive(("bd", step - 1), down_in.at[step - 2], z_down)
            total = total + down_in[step - 2].astype(F32)
        down_out[step - 1] = total.astype(BF16)
        plan.send(("bd", step), down_out.at[step - 1], down_in.at[step - 1], z_down)

    def back_up(step):
        slot = slot_down(downs + 1 - step)
        total = partial[slot]
        if step > 1:
            plan.arrive(("bu", step - 1), up_in.at[step - 2], z_up)
            total = total + up_in[step - 2].astype(F32)
        up_out[step - 1] = total.astype(BF16)
        plan.send(("bu", step), up_out.at[step - 1], up_in.at[step - 1], z_up)

    back_steps = iter(range(1, ups + 1))

    def back():
        step = next(back_steps, None)
        if step is None:
            return
        back_down(step)
        if step <= downs:
            back_up(step)

    def image_partial(core_at, half_at):
        every = texts[...].reshape(blocks * rows, width)
        total = lax.dot_general(
            dlogits[core_at, half_at], every, (((0,), (0,)), ((), ())), preferred_element_type=F32
        )
        return total.reshape(RING, RING, rows, width)

    back()
    for half_at in range(HALVES):
        core_out[half_at] = image_partial(other_core, half_at).astype(BF16)
        plan.send(("c", half_at), core_out.at[half_at], core_in.at[half_at], sibling)
    back()
    for half_at in range(HALVES):
        held[half_at] = image_partial(core, half_at)

    outer_at = (x, y)
    inner_at = (y, x)
    outer_next, outer_prev = (x_next, y_next), (x_prev, y_prev)
    inner_up, inner_down = (y_next, x_next), (y_prev, x_prev)

    def summed(half_at, outer, first=0, last=RING):
        return held[half_at, outer, first:last] + core_in[half_at, outer, first:last].astype(F32)

    def outer_start(half_at):
        plan.arrive(("c", half_at), core_in.at[half_at], sibling)
        at = outer_at[half_at]
        far, near, back_at = ring(at, 2), ring(at, 1), ring(at, -1)
        nxt, prv = outer_next[half_at], outer_prev[half_at]
        outer_out[half_at, far] = summed(half_at, far).astype(BF16)
        plan.send(("o1n", half_at), outer_out.at[half_at, far, 0:2], first_next.at[half_at], nxt)
        plan.send(("o1p", half_at), outer_out.at[half_at, far, 2:4], first_prev.at[half_at], prv)
        outer_out[half_at, near, 2:4] = summed(half_at, near, 2, 4).astype(BF16)
        plan.send(("o2n", half_at, 1), outer_out.at[half_at, near, 2:4], last_next.at[half_at, 2:4], nxt)
        outer_out[half_at, back_at, 0:2] = summed(half_at, back_at, 0, 2).astype(BF16)
        plan.send(("o2p", half_at, 0), outer_out.at[half_at, back_at, 0:2], last_prev.at[half_at, 0:2], prv)

    def outer_second(half_at):
        at = outer_at[half_at]
        near, back_at = ring(at, 1), ring(at, -1)
        nxt, prv = outer_next[half_at], outer_prev[half_at]
        plan.arrive(("o1n", half_at), first_next.at[half_at], nxt)
        outer_out[half_at, near, 0:2] = (summed(half_at, near, 0, 2) + first_next[half_at].astype(F32)).astype(BF16)
        plan.send(("o2n", half_at, 0), outer_out.at[half_at, near, 0:2], last_next.at[half_at, 0:2], nxt)
        plan.arrive(("o1p", half_at), first_prev.at[half_at], prv)
        outer_out[half_at, back_at, 2:4] = (summed(half_at, back_at, 2, 4) + first_prev[half_at].astype(F32)).astype(BF16)
        plan.send(("o2p", half_at, 1), outer_out.at[half_at, back_at, 2:4], last_prev.at[half_at, 2:4], prv)

    def inner_start(half_at):
        nxt, prv = outer_next[half_at], outer_prev[half_at]
        for part in (1, 0):
            rng = slice(2 * part, 2 * part + 2)
            plan.arrive(("o2n", half_at, part), last_next.at[half_at, rng], nxt)
            plan.arrive(("o2p", half_at, 1 - part), last_prev.at[half_at, 2 - 2 * part : 4 - 2 * part], prv)
        total = summed(half_at, outer_at[half_at])
        total = total + last_next[half_at].astype(F32) + last_prev[half_at].astype(F32)
        inner_sum[half_at] = total
        at = inner_at[half_at]
        step = 1 if half_at == 0 else -1
        ahead = inner_up[half_at] if half_at == 0 else inner_down[half_at]
        behind = inner_down[half_at] if half_at == 0 else inner_up[half_at]
        inner_out[half_at] = total.astype(BF16)
        plan.send(("i1", half_at), inner_out.at[half_at, ring(at, 2)], inner_first.at[half_at], ahead)
        plan.send(("i2b", half_at), inner_out.at[half_at, ring(at, -step)], inner_prev.at[half_at], behind)

    def inner_second(half_at):
        at = inner_at[half_at]
        step = 1 if half_at == 0 else -1
        ahead = inner_up[half_at] if half_at == 0 else inner_down[half_at]
        near = ring(at, step)
        plan.arrive(("i1", half_at), inner_first.at[half_at], ahead)
        inner_out[half_at, near] = (inner_sum[half_at, near] + inner_first[half_at].astype(F32)).astype(BF16)
        plan.send(("i2a", half_at), inner_out.at[half_at, near], inner_next.at[half_at], ahead)

    def inner_end(half_at):
        ahead = inner_up[half_at] if half_at == 0 else inner_down[half_at]
        behind = inner_down[half_at] if half_at == 0 else inner_up[half_at]
        plan.arrive(("i2b", half_at), inner_prev.at[half_at], behind)
        plan.arrive(("i2a", half_at), inner_next.at[half_at], ahead)
        total = inner_sum[half_at, inner_at[half_at]]
        total = total + inner_prev[half_at].astype(F32) + inner_next[half_at].astype(F32)
        half_sum[half_at] = total
        half_out[half_at] = total.astype(BF16)

    back()
    outer_start(0)
    outer_start(1)
    back()
    outer_second(0)
    outer_second(1)
    back()
    inner_start(0)
    inner_start(1)
    back()
    inner_second(0)
    inner_second(1)
    back()
    inner_end(0)
    inner_end(1)
    plan.send(("h",), half_out.at[1 - z_half], half_in, z_far)
    for _ in range(ups):
        back()

    plan.arrive(("bd", ups), down_in.at[ups - 1], z_down)
    total = partial[0] + down_in[ups - 1].astype(F32)
    if downs >= 1:
        plan.arrive(("bu", downs), up_in.at[downs - 1], z_up)
        total = total + up_in[downs - 1].astype(F32)
    unit_text, text_scaling = unit_rows(text_ref[...])
    grad_text_ref[...] = unit_backward(unit_text, text_scaling, scale * total)

    own_row = pl.multiple_of(((y * HALVES + z_half) * CORES + core) * rows, rows)
    unit_image, image_scaling = unit_rows(image_ref[pl.ds(own_row, rows), :])
    plan.arrive(("h",), half_in, z_far)
    total = half_sum[z_half] + half_in[...].astype(F32)
    grad_image_ref[...] = unit_backward(unit_image, image_scaling, scale * total)
    plan.finish()


def per_device(image_embed, text_embed, logit_scale, logit_bias):
    rows, width = text_embed.shape
    zlo_size = lax.axis_size("loss") // RING
    blocks = zlo_size
    ups = blocks // 2
    downs = max(blocks - 1 - ups, 1)
    group = RING * RING * rows

    def scratch(*shape, dtype=BF16):
        return pltpu.VMEM((*shape, rows, width), dtype)

    smem = pl.BlockSpec(memory_space=pltpu.SMEM)
    vmem = pl.BlockSpec(memory_space=pltpu.VMEM)
    return pl.pallas_call(
        functools.partial(kernel, zlo_size),
        out_shape=[jax.ShapeDtypeStruct((rows, width), F32)] * 2,
        in_specs=[smem, smem, vmem, vmem],
        out_specs=[vmem, vmem],
        scratch_shapes=[
            scratch(CORES, HALVES, RING, RING),
            scratch(blocks),
            pltpu.VMEM((CORES, HALVES, blocks * rows, group), BF16),
            scratch(blocks, dtype=F32),
            scratch(downs),
            scratch(downs),
            scratch(ups),
            scratch(ups),
            scratch(HALVES, RING, RING),
            scratch(HALVES, RING, RING),
            scratch(HALVES, RING, RING, dtype=F32),
            scratch(HALVES, RING, RING),
            scratch(HALVES, 2),
            scratch(HALVES, 2),
            scratch(HALVES, RING),
            scratch(HALVES, RING),
            scratch(HALVES, RING, dtype=F32),
            scratch(HALVES, RING),
            scratch(HALVES),
            scratch(HALVES),
            scratch(HALVES),
            scratch(HALVES, dtype=F32),
            scratch(HALVES),
            scratch(),
            pltpu.SemaphoreType.DMA((MOST_COPIES,)),
            pltpu.SemaphoreType.DMA((MOST_COPIES,)),
        ],
        compiler_params=pltpu.CompilerParams(
            collective_id=0, has_side_effects=True, vmem_limit_bytes=48 * 1024 * 1024
        ),
    )(logit_scale.reshape(1, 1), logit_bias.reshape(1, 1), image_embed, text_embed)


def solution(mesh):
    placed = (P("loss", None), P(("loss", "section", "mp"), None), P(), P())
    return jax.shard_map(
        per_device,
        mesh=mesh,
        in_specs=placed,
        out_specs=(P(("loss", "section", "mp"), None), P(("loss", "section", "mp"), None)),
        check_vma=False,
    )
```

```python
import functools

import jax
import jax.numpy as jnp
from jax import lax
from jax.experimental import pallas as pl
from jax.experimental.pallas import tpu as pltpu
from jax.sharding import PartitionSpec as P

epsilon = 1e-06
MESH = pl.DeviceIdType.MESH
F32 = jnp.float32
BF16 = jnp.bfloat16

RING = 4
HALVES = 2
CORES = 2
MOST_COPIES = 112

TREE = {0: (3, 1), 3: (6, 4), 1: (2,), 6: (8, 7), 4: (5,)}

X_OWN, X_PREV, X_NEXT, X_FAR = range(4)
Y_OWN, Y_NEXT, Y_FAR, Y_PREV = range(4)


def unit_rows(values):
    widened = values.astype(F32)
    scaling = lax.rsqrt(jnp.sum(widened * widened, axis=-1, keepdims=True) + epsilon)
    return (widened * scaling, scaling)


def unit_backward(unit, scaling, gradient):
    return (gradient - unit * jnp.sum(unit * gradient, axis=-1, keepdims=True)) * scaling


class Plan:
    def __init__(self, send_sems, recv_sems):
        self.send_sems = send_sems
        self.recv_sems = recv_sems
        self.numbers = {}
        self.sends = []

    def copy(self, key, source, target, device):
        at = self.numbers.setdefault(key, len(self.numbers))
        return pltpu.make_async_remote_copy(
            src_ref=source,
            dst_ref=target,
            send_sem=self.send_sems.at[at],
            recv_sem=self.recv_sems.at[at],
            device_id=device,
            device_id_type=MESH,
        )

    def send(self, key, source, target, device):
        copy = self.copy(key, source, target, device)
        copy.start()
        self.sends.append(copy)

    def arrive(self, key, target, device):
        self.copy(key, target, target, device).wait_recv()

    def finish(self):
        for copy in self.sends:
            copy.wait_send()


class Spread:
    def __init__(self, blocks):
        self.reach = (blocks // 2, blocks - 1 - blocks // 2)
        self.parent = {}
        self.levels = []
        level = [0]
        while level:
            found = []
            for at in level:
                for child in TREE.get(at, ()):
                    if child <= max(self.reach):
                        self.parent[child] = at
                        found.append(child)
            level = found
            if found:
                self.levels.append(found)
        self.slots = {(0, 0): 0, (1, 0): 0}
        self.order = []
        for level in self.levels:
            for at in level:
                for way in range(2):
                    if at <= self.reach[way]:
                        self.slots[way, at] = len(self.order) + 1
                        self.order.append((way, at))
        self.lengths = sorted({child - at for child, at in self.parent.items()})

    def children(self, way, at):
        return [child for child in TREE.get(at, ()) if child <= self.reach[way]]


def kernel(
    zlo_size,
    scale_ref,
    bias_ref,
    image_hbm,
    text_hbm,
    grad_image_ref,
    grad_text_ref,
    image_raw,
    text_raw,
    images,
    texts,
    dlogits,
    partial,
    back_out,
    back_in,
    core_out,
    core_in,
    held,
    outer_out,
    first_next,
    first_prev,
    last_next,
    last_prev,
    inner_out,
    inner_in,
    half_sum,
    half_out,
    half_in,
    load_sems,
    send_sems,
    recv_sems,
):
    rows, width = text_raw.shape
    blocks = zlo_size
    spread = Spread(blocks)
    side = RING * CORES * RING * rows
    z_size = zlo_size * HALVES

    loss = lax.axis_index("loss")
    y = lax.axis_index("section")
    mp = lax.axis_index("mp")
    z_lo = lax.div(loss, RING)
    x = lax.rem(loss, RING)
    z_half = lax.div(mp, CORES)
    core = lax.rem(mp, CORES)
    z = z_half * zlo_size + z_lo

    def device(x_steps=0, y_steps=0, z_steps=0, core_steps=0):
        z_at = lax.rem(z + (z_steps + z_size), z_size)
        return {
            "loss": lax.rem(z_at, zlo_size) * RING + lax.rem(x + (x_steps + RING), RING),
            "section": lax.rem(y + (y_steps + RING), RING),
            "mp": lax.div(z_at, zlo_size) * CORES + lax.rem(core + core_steps, CORES),
        }

    z_far = device(z_steps=zlo_size)
    x_next, x_prev, x_far = device(x_steps=1), device(x_steps=-1), device(x_steps=2)
    y_next, y_prev, y_far = device(y_steps=1), device(y_steps=-1), device(y_steps=2)
    sibling = device(core_steps=1)
    along_z = {steps: device(z_steps=steps) for length in spread.lengths for steps in (length, -length)}
    neighbours = [*along_z.values(), x_next, x_prev, x_far, y_next, y_prev, y_far, sibling]

    barrier = pltpu.get_barrier_semaphore()
    for neighbour in neighbours:
        pl.semaphore_signal(barrier, inc=1, device_id=neighbour, device_id_type=MESH)

    load_text = pltpu.make_async_copy(text_hbm, text_raw, load_sems.at[0])
    load_image = pltpu.make_async_copy(image_hbm, image_raw, load_sems.at[1])
    load_text.start()
    load_image.start()

    plan = Plan(send_sems, recv_sems)
    load_text.wait()
    texts[0] = unit_rows(text_raw[...])[0].astype(BF16)

    load_image.wait()

    def normalize(core_steps):
        for half_at in range(HALVES):
            for y_steps in range(RING):
                y_at = lax.rem(y + y_steps, RING)
                half = z_half if half_at == 1 else 1 - z_half
                core_at = lax.rem(core + core_steps, CORES)
                start = pl.multiple_of(((y_at * HALVES + half) * CORES + core_at) * rows, rows)
                low = unit_rows(image_raw[pl.ds(start, rows), :])[0].astype(BF16)
                images[X_OWN, half_at, core_steps, y_steps] = low

    normalize(0)
    pl.semaphore_wait(barrier, len(neighbours))

    def pass_on(way, at):
        for child in spread.children(way, at):
            target = along_z[child - at if way == 0 else at - child]
            source, slot = spread.slots[way, at], spread.slots[way, child]
            plan.send(("t", way, child), texts.at[source], texts.at[slot], target)

    def text_level(level):
        for at in spread.levels[level]:
            for way in range(2):
                if at <= spread.reach[way]:
                    near = spread.lengths[0] * (1 - 2 * way)
                    plan.arrive(("t", way, at), texts.at[spread.slots[way, at]], along_z[near])
                    pass_on(way, at)

    pass_on(0, 0)
    pass_on(1, 0)

    for half_at in range(HALVES):
        own = images.at[X_OWN, half_at, 0]
        plan.send(("xn", half_at), own, images.at[X_PREV, half_at, 0], x_next)
        other = 1 - half_at
        own = images.at[X_OWN, other, 0]
        plan.send(("xp", other), own, images.at[X_NEXT, other, 0], x_prev)

    normalize(1)

    def to_sibling(x_at, half_at):
        mine, theirs = images.at[x_at, half_at, 0], images.at[x_at, half_at, 1]
        plan.send(("xc", x_at, half_at), mine, theirs, sibling)

    def image_near(half_at):
        other = 1 - half_at
        from_prev, from_next = images.at[X_PREV, half_at, 0], images.at[X_NEXT, other, 0]
        plan.arrive(("xn", half_at), from_prev, x_next)
        if half_at == 0:
            plan.send(("xf", 0), from_prev, images.at[X_FAR, 0, 0], x_next)
        plan.arrive(("xp", other), from_next, x_prev)
        if half_at == 0:
            plan.send(("xf", 1), from_next, images.at[X_FAR, 1, 0], x_prev)
        to_sibling(X_PREV, half_at)
        to_sibling(X_NEXT, other)

    def image_far():
        for half_at in range(HALVES):
            plan.arrive(("xf", half_at), images.at[X_FAR, half_at, 0], x_next)
            to_sibling(X_FAR, half_at)

    def from_sibling(*x_ats):
        for half_at in range(HALVES):
            for x_at in x_ats:
                plan.arrive(("xc", x_at, half_at), images.at[x_at, half_at, 1], sibling)

    scale = scale_ref[0, 0]
    bias = bias_ref[0, 0]
    per_x = HALVES * CORES * RING * rows
    per_half = CORES * RING * rows

    def batch(first, last):
        count = (last - first) * per_x
        block = texts[...].reshape(blocks * rows, width)
        every = images[first:last].reshape(count, width)
        logits = scale * lax.dot_general(
            block, every, (((1,), (1,)), ((), ())), preferred_element_type=F32
        )
        slope = jax.nn.sigmoid(logits + bias)
        if first == X_OWN:
            text_ids = lax.broadcasted_iota(jnp.int32, slope.shape, 0)
            image_ids = lax.broadcasted_iota(jnp.int32, slope.shape, 1)
            positive = (text_ids < rows) & (image_ids == text_ids + per_half)
            slope = slope - jnp.where(positive, 1.0, 0.0)
        low = slope.astype(BF16)
        for x_at in range(first, last):
            for half_at in range(HALVES):
                start = (x_at - first) * per_x + half_at * per_half
                dlogits[half_at, :, x_at * per_half : (x_at + 1) * per_half] = low[:, start : start + per_half]
        grads = jnp.dot(low, every, preferred_element_type=F32).reshape(blocks, rows, width)
        if first == X_OWN:
            partial[...] = grads
        else:
            partial[...] += grads

    text_level(0)
    image_near(0)
    for level in range(1, len(spread.levels)):
        text_level(level)
        if level == 1:
            image_near(1)
    image_far()
    from_sibling(X_PREV, X_NEXT)
    batch(X_OWN, X_FAR)
    from_sibling(X_FAR)
    batch(X_FAR, X_FAR + 1)

    def back(level):
        for at in reversed(spread.levels[level]):
            for way in range(2):
                if at <= spread.reach[way]:
                    slot = spread.slots[way, at]
                    total = partial[slot]
                    for child in spread.children(way, at):
                        total = total + back_arrival(way, child)
                    back_out[slot] = total.astype(BF16)
                    length = at - spread.parent[at]
                    target = along_z[length if way == 1 else -length]
                    plan.send(("b", way, at), back_out.at[slot], back_in.at[slot], target)

    def back_arrival(way, child):
        slot = spread.slots[way, child]
        near = spread.lengths[0] * (2 * way - 1)
        plan.arrive(("b", way, child), back_in.at[slot], along_z[near])
        return back_in[slot].astype(F32)

    def image_partial(half_at):
        every = texts[...].reshape(blocks * rows, width)
        total = lax.dot_general(
            dlogits[half_at], every, (((0,), (0,)), ((), ())), preferred_element_type=F32
        )
        total = total.reshape(RING, CORES, RING, rows, width)
        core_out[half_at] = total[:, 1].astype(BF16)
        plan.send(("c", half_at), core_out.at[half_at], core_in.at[half_at], sibling)
        held[half_at] = total[:, 0]

    split = (width // 128 + 1) // 2 * 128
    columns = (slice(0, split), slice(split, width))
    ahead, behind = (x_next, y_next), (x_prev, y_prev)
    positions = ((X_OWN, X_NEXT, X_FAR, X_PREV), (Y_OWN, Y_NEXT, Y_FAR, Y_PREV))

    def at_block(half_at, part, outer, first=0, last=RING):
        if part == 0:
            return (half_at, outer, slice(first, last), slice(None), columns[0])
        return (half_at, slice(first, last), outer, slice(None), columns[1])

    def at_line(half_at, part, first=0, last=RING):
        return (half_at, slice(first, last), slice(None), columns[part])

    def send_block(key, half_at, part, outer, first, last, target, target_at, to):
        source = outer_out.at[at_block(half_at, part, outer, first, last)]
        plan.send((key, half_at, part, first), source, target.at[target_at], to)

    def summed(index):
        return held[index] + core_in[index].astype(F32)

    def outer_start(half_at):
        plan.arrive(("c", half_at), core_in.at[half_at], sibling)
        for part in range(2):
            _, nxt, far, prv = positions[part]
            index = at_block(half_at, part, far)
            outer_out[index] = summed(index).astype(BF16)
            line = at_line(half_at, part, 0, 2)
            send_block("o1n", half_at, part, far, 0, 2, first_next, line, ahead[part])
            send_block("o1p", half_at, part, far, 2, 4, first_prev, line, behind[part])
        for part in range(2):
            _, nxt, far, prv = positions[part]
            index = at_block(half_at, part, nxt, 2, 4)
            outer_out[index] = summed(index).astype(BF16)
            send_block("o2n", half_at, part, nxt, 2, 4, last_next, at_line(half_at, part, 2, 4), ahead[part])
            index = at_block(half_at, part, prv, 0, 2)
            outer_out[index] = summed(index).astype(BF16)
            send_block("o2p", half_at, part, prv, 0, 2, last_prev, at_line(half_at, part, 0, 2), behind[part])

    def outer_second(half_at):
        for part in range(2):
            _, nxt, far, prv = positions[part]
            line = at_line(half_at, part, 0, 2)
            plan.arrive(("o1n", half_at, part, 0), first_next.at[line], ahead[part])
            index = at_block(half_at, part, nxt, 0, 2)
            outer_out[index] = (summed(index) + first_next[line].astype(F32)).astype(BF16)
            send_block("o2n", half_at, part, nxt, 0, 2, last_next, line, ahead[part])
            plan.arrive(("o1p", half_at, part, 2), first_prev.at[line], behind[part])
            index = at_block(half_at, part, prv, 2, 4)
            outer_out[index] = (summed(index) + first_prev[line].astype(F32)).astype(BF16)
            send_block("o2p", half_at, part, prv, 2, 4, last_prev, at_line(half_at, part, 2, 4), behind[part])

    inner_targets = (
        ((Y_FAR, y_far), (Y_NEXT, y_next), (Y_PREV, y_prev)),
        ((X_FAR, x_far), (X_NEXT, x_next), (X_PREV, x_prev)),
    )

    def inner_start(half_at):
        for part in range(2):
            for first in (2, 0):
                line = at_line(half_at, part, first, first + 2)
                plan.arrive(("o2n", half_at, part, first), last_next.at[line], ahead[part])
            for first in (0, 2):
                line = at_line(half_at, part, first, first + 2)
                plan.arrive(("o2p", half_at, part, first), last_prev.at[line], behind[part])
            line = at_line(half_at, part)
            total = summed(at_block(half_at, part, 0))
            total = total + last_next[line].astype(F32) + last_prev[line].astype(F32)
            inner_out[line] = total.astype(BF16)
            for at, to in inner_targets[part]:
                block = (half_at, at, slice(None), columns[part])
                plan.send(("i", half_at, part, at), inner_out.at[block], inner_in.at[block], to)
            half_sum[half_at, :, columns[part]] = total[0]

    def inner_end(half_at):
        for part in range(2):
            total = half_sum[half_at, :, columns[part]]
            for at, to in inner_targets[part]:
                block = (half_at, at, slice(None), columns[part])
                plan.arrive(("i", half_at, part, at), inner_in.at[block], to)
                total = total + inner_in[block].astype(F32)
            if half_at == 0:
                half_out[:, columns[part]] = total.astype(BF16)
            else:
                half_sum[half_at, :, columns[part]] = total

    last = len(spread.levels) - 1
    back(last)
    image_partial(0)
    image_partial(1)
    outer_start(0)
    for level in range(last - 1, 0, -1):
        back(level)
    outer_second(0)
    outer_start(1)
    if last > 0:
        back(0)
    inner_start(0)
    outer_second(1)

    total = partial[0]
    for way in range(2):
        for child in spread.children(way, 0):
            total = total + back_arrival(way, child)
    inner_end(0)
    plan.send(("h",), half_out, half_in, z_far)
    unit_text, text_scaling = unit_rows(text_raw[...])
    grad_text_ref[...] = unit_backward(unit_text, text_scaling, scale * total)

    inner_start(1)
    inner_end(1)
    own_row = pl.multiple_of(((y * HALVES + z_half) * CORES + core) * rows, rows)
    unit_image, image_scaling = unit_rows(image_raw[pl.ds(own_row, rows), :])
    plan.arrive(("h",), half_in, z_far)
    total = half_sum[1] + half_in[...].astype(F32)
    grad_image_ref[...] = unit_backward(unit_image, image_scaling, scale * total)
    plan.finish()


def per_device(image_embed, text_embed, logit_scale, logit_bias):
    rows, width = text_embed.shape
    zlo_size = lax.axis_size("loss") // RING
    blocks = zlo_size

    def scratch(*shape, dtype=BF16):
        return pltpu.VMEM((*shape, rows, width), dtype)

    smem = pl.BlockSpec(memory_space=pltpu.SMEM)
    vmem = pl.BlockSpec(memory_space=pltpu.VMEM)
    anywhere = pl.BlockSpec(memory_space=pl.ANY)
    return pl.pallas_call(
        functools.partial(kernel, zlo_size),
        out_shape=[jax.ShapeDtypeStruct((rows, width), F32)] * 2,
        in_specs=[smem, smem, anywhere, anywhere],
        out_specs=[vmem, vmem],
        scratch_shapes=[
            pltpu.VMEM(image_embed.shape, BF16),
            pltpu.VMEM(text_embed.shape, BF16),
            scratch(RING, HALVES, CORES, RING),
            scratch(blocks),
            pltpu.VMEM((HALVES, blocks * rows, RING * CORES * RING * rows), BF16),
            scratch(blocks, dtype=F32),
            scratch(blocks),
            scratch(blocks),
            scratch(HALVES, RING, RING),
            scratch(HALVES, RING, RING),
            scratch(HALVES, RING, RING, dtype=F32),
            scratch(HALVES, RING, RING),
            scratch(HALVES, 2),
            scratch(HALVES, 2),
            scratch(HALVES, RING),
            scratch(HALVES, RING),
            scratch(HALVES, RING),
            scratch(HALVES, RING),
            scratch(HALVES, dtype=F32),
            scratch(),
            scratch(),
            pltpu.SemaphoreType.DMA((2,)),
            pltpu.SemaphoreType.DMA((MOST_COPIES,)),
            pltpu.SemaphoreType.DMA((MOST_COPIES,)),
        ],
        compiler_params=pltpu.CompilerParams(
            collective_id=0, has_side_effects=True, vmem_limit_bytes=60 * 1024 * 1024
        ),
    )(logit_scale.reshape(1, 1), logit_bias.reshape(1, 1), image_embed, text_embed)


def solution(mesh):
    placed = (P("loss", None), P(("loss", "section", "mp"), None), P(), P())
    return jax.shard_map(
        per_device,
        mesh=mesh,
        in_specs=placed,
        out_specs=(P(("loss", "section", "mp"), None), P(("loss", "section", "mp"), None)),
        check_vma=False,
    )
```

```python
import functools

import jax
import jax.numpy as jnp
from jax import lax
from jax.experimental import pallas as pl
from jax.experimental.pallas import tpu as pltpu
from jax.sharding import PartitionSpec as P

epsilon = 1e-06
MESH = pl.DeviceIdType.MESH
F32 = jnp.float32
BF16 = jnp.bfloat16

RING = 4
HALVES = 2
CORES = 2
MOST_COPIES = 112

TREE = {0: (3, 1), 3: (6, 4), 1: (2,), 6: (8, 7), 4: (5,)}

X_OWN, X_PREV, X_NEXT, X_FAR = range(4)
Y_OWN, Y_NEXT, Y_FAR, Y_PREV = range(4)


def unit_rows(values):
    widened = values.astype(F32)
    scaling = lax.rsqrt(jnp.sum(widened * widened, axis=-1, keepdims=True) + epsilon)
    return (widened * scaling, scaling)


def unit_backward(unit, scaling, gradient):
    return (gradient - unit * jnp.sum(unit * gradient, axis=-1, keepdims=True)) * scaling


class Plan:
    def __init__(self, send_sems, recv_sems):
        self.send_sems = send_sems
        self.recv_sems = recv_sems
        self.numbers = {}
        self.sends = []

    def copy(self, key, source, target, device):
        at = self.numbers.setdefault(key, len(self.numbers))
        return pltpu.make_async_remote_copy(
            src_ref=source,
            dst_ref=target,
            send_sem=self.send_sems.at[at],
            recv_sem=self.recv_sems.at[at],
            device_id=device,
            device_id_type=MESH,
        )

    def send(self, key, source, target, device):
        copy = self.copy(key, source, target, device)
        copy.start()
        self.sends.append(copy)

    def arrive(self, key, target, device):
        self.copy(key, target, target, device).wait_recv()

    def finish(self):
        for copy in self.sends:
            copy.wait_send()


class Spread:
    def __init__(self, blocks):
        self.reach = (blocks // 2, blocks - 1 - blocks // 2)
        self.parent = {}
        self.levels = []
        level = [0]
        while level:
            found = []
            for at in level:
                for child in TREE.get(at, ()):
                    if child <= max(self.reach):
                        self.parent[child] = at
                        found.append(child)
            level = found
            if found:
                self.levels.append(found)
        self.slots = {(0, 0): 0, (1, 0): 0}
        self.order = []
        for level in self.levels:
            for at in level:
                for way in range(2):
                    if at <= self.reach[way]:
                        self.slots[way, at] = len(self.order) + 1
                        self.order.append((way, at))
        self.lengths = sorted({child - at for child, at in self.parent.items()})

    def children(self, way, at):
        return [child for child in TREE.get(at, ()) if child <= self.reach[way]]


def kernel(
    zlo_size,
    scale_ref,
    bias_ref,
    image_hbm,
    text_hbm,
    grad_image_ref,
    grad_text_ref,
    image_raw,
    text_raw,
    images,
    texts,
    dlogits,
    partial,
    back_out,
    back_in,
    core_out,
    core_in,
    held,
    outer_out,
    outer_in,
    inner_out,
    inner_in,
    half_sum,
    half_out,
    half_in,
    load_sems,
    token_sems,
    send_sems,
    recv_sems,
):
    rows, width = text_raw.shape
    blocks = zlo_size
    spread = Spread(blocks)
    side = RING * CORES * RING * rows
    z_size = zlo_size * HALVES

    loss = lax.axis_index("loss")
    y = lax.axis_index("section")
    mp = lax.axis_index("mp")
    z_lo = lax.div(loss, RING)
    x = lax.rem(loss, RING)
    z_half = lax.div(mp, CORES)
    core = lax.rem(mp, CORES)
    z = z_half * zlo_size + z_lo

    def device(x_steps=0, y_steps=0, z_steps=0, core_steps=0):
        z_at = lax.rem(z + (z_steps + z_size), z_size)
        return {
            "loss": lax.rem(z_at, zlo_size) * RING + lax.rem(x + (x_steps + RING), RING),
            "section": lax.rem(y + (y_steps + RING), RING),
            "mp": lax.div(z_at, zlo_size) * CORES + lax.rem(core + core_steps, CORES),
        }

    z_far = device(z_steps=zlo_size)
    x_next, x_prev, x_far = device(x_steps=1), device(x_steps=-1), device(x_steps=2)
    y_next, y_prev, y_far = device(y_steps=1), device(y_steps=-1), device(y_steps=2)
    sibling = device(core_steps=1)
    along_z = {steps: device(z_steps=steps) for length in spread.lengths for steps in (length, -length)}
    neighbours = [*along_z.values(), x_next, x_prev, x_far, y_next, y_prev, y_far, sibling]

    barrier = pltpu.get_barrier_semaphore()
    for neighbour in neighbours:
        pl.semaphore_signal(barrier, inc=1, device_id=neighbour, device_id_type=MESH)

    load_text = pltpu.make_async_copy(text_hbm, text_raw, load_sems.at[0])
    load_image = pltpu.make_async_copy(image_hbm, image_raw, load_sems.at[1])
    load_text.start()
    load_image.start()

    plan = Plan(send_sems, recv_sems)
    load_text.wait()
    texts[0] = unit_rows(text_raw[...])[0].astype(BF16)

    def normalize(core_steps):
        for half_at in range(HALVES):
            for y_steps in range(RING):
                y_at = lax.rem(y + y_steps, RING)
                half = z_half if half_at == 1 else 1 - z_half
                core_at = lax.rem(core + core_steps, CORES)
                start = pl.multiple_of(((y_at * HALVES + half) * CORES + core_at) * rows, rows)
                low = unit_rows(image_raw[pl.ds(start, rows), :])[0].astype(BF16)
                images[X_OWN, half_at, core_steps, y_steps] = low

    pl.semaphore_wait(barrier, len(neighbours))

    def pass_on(way, at):
        for child in spread.children(way, at):
            target = along_z[child - at if way == 0 else at - child]
            source, slot = spread.slots[way, at], spread.slots[way, child]
            plan.send(("t", way, child), texts.at[source], texts.at[slot], target)

    def text_level(level):
        for at in spread.levels[level]:
            for way in range(2):
                if at <= spread.reach[way]:
                    near = spread.lengths[0] * (1 - 2 * way)
                    plan.arrive(("t", way, at), texts.at[spread.slots[way, at]], along_z[near])
                    pass_on(way, at)

    pass_on(0, 0)
    pass_on(1, 0)
    load_image.wait()
    normalize(0)

    for half_at in range(HALVES):
        own = images.at[X_OWN, half_at, 0]
        plan.send(("xn", half_at), own, images.at[X_PREV, half_at, 0], x_next)
        other = 1 - half_at
        own = images.at[X_OWN, other, 0]
        plan.send(("xp", other), own, images.at[X_NEXT, other, 0], x_prev)

    normalize(1)

    def to_sibling(x_at, half_at):
        mine, theirs = images.at[x_at, half_at, 0], images.at[x_at, half_at, 1]
        plan.send(("xc", x_at, half_at), mine, theirs, sibling)

    def image_near(half_at):
        other = 1 - half_at
        from_prev, from_next = images.at[X_PREV, half_at, 0], images.at[X_NEXT, other, 0]
        plan.arrive(("xn", half_at), from_prev, x_next)
        if half_at == 0:
            plan.send(("xf", 0), from_prev, images.at[X_FAR, 0, 0], x_next)
        plan.arrive(("xp", other), from_next, x_prev)
        if half_at == 0:
            plan.send(("xf", 1), from_next, images.at[X_FAR, 1, 0], x_prev)
        to_sibling(X_PREV, half_at)
        to_sibling(X_NEXT, other)

    def image_far():
        for half_at in range(HALVES):
            plan.arrive(("xf", half_at), images.at[X_FAR, half_at, 0], x_next)
            to_sibling(X_FAR, half_at)

    def from_sibling(*x_ats):
        for half_at in range(HALVES):
            for x_at in x_ats:
                plan.arrive(("xc", x_at, half_at), images.at[x_at, half_at, 1], sibling)

    scale = scale_ref[0, 0]
    bias = bias_ref[0, 0]
    per_x = HALVES * CORES * RING * rows
    per_half = CORES * RING * rows

    def batch(slots, first, last):
        count = (last - first) * per_x
        low_row, high_row = slots[0] * rows, slots[1] * rows
        block = texts[slots[0] : slots[1]].reshape(high_row - low_row, width)
        every = images[first:last].reshape(count, width)
        logits = scale * lax.dot_general(
            block, every, (((1,), (1,)), ((), ())), preferred_element_type=F32
        )
        slope = jax.nn.sigmoid(logits + bias)
        if first == X_OWN and slots[0] == 0:
            text_ids = lax.broadcasted_iota(jnp.int32, slope.shape, 0)
            image_ids = lax.broadcasted_iota(jnp.int32, slope.shape, 1)
            positive = (text_ids < rows) & (image_ids == text_ids + per_half)
            slope = slope - jnp.where(positive, 1.0, 0.0)
        low = slope.astype(BF16)
        for x_at in range(first, last):
            for half_at in range(HALVES):
                start = (x_at - first) * per_x + half_at * per_half
                part = low[:, start : start + per_half]
                dlogits[half_at, low_row:high_row, x_at * per_half : (x_at + 1) * per_half] = part
        grads = jnp.dot(low, every, preferred_element_type=F32).reshape(-1, rows, width)
        if first == X_OWN:
            partial[slots[0] : slots[1]] = grads
        else:
            partial[slots[0] : slots[1]] += grads

    def back(level):
        for at in reversed(spread.levels[level]):
            for way in range(2):
                if at <= spread.reach[way]:
                    slot = spread.slots[way, at]
                    total = partial[slot]
                    for child in spread.children(way, at):
                        total = total + back_arrival(way, child)
                    back_out[slot] = total.astype(BF16)
                    length = at - spread.parent[at]
                    target = along_z[length if way == 1 else -length]
                    plan.send(("b", way, at), back_out.at[slot], back_in.at[slot], target)

    def back_arrival(way, child):
        slot = spread.slots[way, child]
        near = spread.lengths[0] * (2 * way - 1)
        plan.arrive(("b", way, child), back_in.at[slot], along_z[near])
        return back_in[slot].astype(F32)

    def image_partial(half_at):
        every = texts[...].reshape(blocks * rows, width)
        total = lax.dot_general(
            dlogits[half_at], every, (((0,), (0,)), ((), ())), preferred_element_type=F32
        )
        total = total.reshape(RING, CORES, RING, rows, width)
        core_out[half_at] = total[:, 1].astype(BF16)
        plan.send(("c", half_at), core_out.at[half_at], core_in.at[half_at], sibling)
        held[half_at] = total[:, 0]

    split = (width // 128 + 1) // 2 * 128
    columns = (slice(0, split), slice(split, width))
    x_targets = ((X_FAR, x_far), (X_NEXT, x_next), (X_PREV, x_prev))
    y_targets = ((Y_FAR, y_far), (Y_NEXT, y_next), (Y_PREV, y_prev))
    outer_targets, inner_targets = (x_targets, y_targets), (y_targets, x_targets)

    def at_block(half_at, part, outer):
        if part == 0:
            return (half_at, outer, slice(None), slice(None), columns[0])
        return (half_at, slice(None), outer, slice(None), columns[1])

    def at_line(half_at, part, *at):
        return (half_at, *at, slice(None), slice(None), columns[part])

    def summed(index):
        return held[index] + core_in[index].astype(F32)

    def outer_start(half_at):
        plan.arrive(("c", half_at), core_in.at[half_at], sibling)
        for way in range(RING - 1):
            for part in range(2):
                at, to = outer_targets[part][way]
                index = at_block(half_at, part, at)
                outer_out[index] = summed(index).astype(BF16)
                plan.send(("o", half_at, part, at), outer_out.at[index], outer_in.at[at_line(half_at, part, at)], to)

    def inner_start(half_at):
        for part in range(2):
            total = summed(at_block(half_at, part, 0))
            for at, to in reversed(outer_targets[part]):
                line = at_line(half_at, part, at)
                plan.arrive(("o", half_at, part, at), outer_in.at[line], to)
                total = total + outer_in[line].astype(F32)
            inner_out[at_line(half_at, part)] = total.astype(BF16)
            for at, to in inner_targets[part]:
                block = (half_at, at, slice(None), columns[part])
                plan.send(("i", half_at, part, at), inner_out.at[block], inner_in.at[block], to)
            half_sum[half_at, :, columns[part]] = total[0]

    def inner_end(half_at, part):
        total = half_sum[half_at, :, columns[part]]
        for at, to in reversed(inner_targets[part]):
            block = (half_at, at, slice(None), columns[part])
            plan.arrive(("i", half_at, part, at), inner_in.at[block], to)
            total = total + inner_in[block].astype(F32)
        if half_at == 0:
            half_out[:, columns[part]] = total.astype(BF16)
        else:
            half_sum[half_at, :, columns[part]] = total

    def give_token(at):
        pl.semaphore_signal(token_sems.at[at], inc=1, device_id=token_target, device_id_type=MESH)

    def take_token(at):
        pl.semaphore_wait(token_sems.at[at], 1)

    token_target = along_z[spread.lengths[-1]]
    last = len(spread.levels) - 1
    cut = min(spread.slots[way, at] for way, at in spread.order if at in spread.levels[last])
    early, late = (0, cut), (cut, blocks)
    for level in range(last):
        text_level(level)
        if level < HALVES:
            image_near(level)
    for level in range(last, HALVES):
        image_near(level)
    image_far()
    from_sibling(X_PREV, X_NEXT)
    batch(early, X_OWN, X_FAR)
    text_level(last)
    give_token(0)
    from_sibling(X_FAR)
    batch(late, X_OWN, X_FAR + 1)
    back(last)
    batch(early, X_FAR, X_FAR + 1)

    image_partial(0)
    image_partial(1)
    take_token(0)
    give_token(1)
    outer_start(0)
    for level in range(last - 1, 0, -1):
        back(level)
    inner_start(0)
    if last > 0:
        back(0)
    inner_end(0, 0)
    inner_end(0, 1)
    take_token(1)
    plan.send(("h",), half_out, half_in, z_far)
    outer_start(1)

    total = partial[0]
    for way in range(2):
        for child in spread.children(way, 0):
            total = total + back_arrival(way, child)
    unit_text, text_scaling = unit_rows(text_raw[...])
    grad_text_ref[...] = unit_backward(unit_text, text_scaling, scale * total)

    inner_start(1)
    inner_end(1, 0)
    inner_end(1, 1)
    own_row = pl.multiple_of(((y * HALVES + z_half) * CORES + core) * rows, rows)
    unit_image, image_scaling = unit_rows(image_raw[pl.ds(own_row, rows), :])
    plan.arrive(("h",), half_in, z_far)
    total = half_sum[1] + half_in[...].astype(F32)
    grad_image_ref[...] = unit_backward(unit_image, image_scaling, scale * total)
    plan.finish()


def per_device(image_embed, text_embed, logit_scale, logit_bias):
    rows, width = text_embed.shape
    zlo_size = lax.axis_size("loss") // RING
    blocks = zlo_size

    def scratch(*shape, dtype=BF16):
        return pltpu.VMEM((*shape, rows, width), dtype)

    smem = pl.BlockSpec(memory_space=pltpu.SMEM)
    vmem = pl.BlockSpec(memory_space=pltpu.VMEM)
    anywhere = pl.BlockSpec(memory_space=pl.ANY)
    return pl.pallas_call(
        functools.partial(kernel, zlo_size),
        out_shape=[jax.ShapeDtypeStruct((rows, width), F32)] * 2,
        in_specs=[smem, smem, anywhere, anywhere],
        out_specs=[vmem, vmem],
        scratch_shapes=[
            pltpu.VMEM(image_embed.shape, BF16),
            pltpu.VMEM(text_embed.shape, BF16),
            scratch(RING, HALVES, CORES, RING),
            scratch(blocks),
            pltpu.VMEM((HALVES, blocks * rows, RING * CORES * RING * rows), BF16),
            scratch(blocks, dtype=F32),
            scratch(blocks),
            scratch(blocks),
            scratch(HALVES, RING, RING),
            scratch(HALVES, RING, RING),
            scratch(HALVES, RING, RING, dtype=F32),
            scratch(HALVES, RING, RING),
            scratch(HALVES, RING, RING),
            scratch(HALVES, RING),
            scratch(HALVES, RING),
            scratch(HALVES, dtype=F32),
            scratch(),
            scratch(),
            pltpu.SemaphoreType.DMA((2,)),
            pltpu.SemaphoreType.REGULAR((2,)),
            pltpu.SemaphoreType.DMA((MOST_COPIES,)),
            pltpu.SemaphoreType.DMA((MOST_COPIES,)),
        ],
        compiler_params=pltpu.CompilerParams(
            collective_id=0, has_side_effects=True, vmem_limit_bytes=60 * 1024 * 1024
        ),
    )(logit_scale.reshape(1, 1), logit_bias.reshape(1, 1), image_embed, text_embed)


def solution(mesh):
    placed = (P("loss", None), P(("loss", "section", "mp"), None), P(), P())
    return jax.shard_map(
        per_device,
        mesh=mesh,
        in_specs=placed,
        out_specs=(P(("loss", "section", "mp"), None), P(("loss", "section", "mp"), None)),
        check_vma=False,
    )
```

```python
import functools

import jax
import jax.numpy as jnp
from jax import lax
from jax.experimental import pallas as pl
from jax.experimental.pallas import tpu as pltpu
from jax.sharding import PartitionSpec as P

epsilon = 1e-06
MESH = pl.DeviceIdType.MESH
F32 = jnp.float32
BF16 = jnp.bfloat16

RING = 4
HALVES = 2
CORES = 2
MOST_COPIES = 112

TREE = {0: (3, 1), 3: (6, 4), 1: (2,), 6: (8, 7), 4: (5,)}

X_OWN, X_PREV, X_NEXT, X_FAR = range(4)
Y_OWN, Y_NEXT, Y_FAR, Y_PREV = range(4)


def unit_rows(values):
    widened = values.astype(F32)
    scaling = lax.rsqrt(jnp.sum(widened * widened, axis=-1, keepdims=True) + epsilon)
    return (widened * scaling, scaling)


def unit_backward(unit, scaling, gradient):
    return (gradient - unit * jnp.sum(unit * gradient, axis=-1, keepdims=True)) * scaling


class Plan:
    def __init__(self, send_sems, recv_sems):
        self.send_sems = send_sems
        self.recv_sems = recv_sems
        self.numbers = {}
        self.sends = []

    def copy(self, key, source, target, device):
        at = self.numbers.setdefault(key, len(self.numbers))
        return pltpu.make_async_remote_copy(
            src_ref=source,
            dst_ref=target,
            send_sem=self.send_sems.at[at],
            recv_sem=self.recv_sems.at[at],
            device_id=device,
            device_id_type=MESH,
        )

    def send(self, key, source, target, device):
        copy = self.copy(key, source, target, device)
        copy.start()
        self.sends.append(copy)

    def arrive(self, key, target, device):
        self.copy(key, target, target, device).wait_recv()

    def finish(self):
        for copy in self.sends:
            copy.wait_send()


class Spread:
    def __init__(self, blocks):
        self.reach = (blocks // 2, blocks - 1 - blocks // 2)
        self.parent = {}
        self.levels = []
        level = [0]
        while level:
            found = []
            for at in level:
                for child in TREE.get(at, ()):
                    if child <= max(self.reach):
                        self.parent[child] = at
                        found.append(child)
            level = found
            if found:
                self.levels.append(found)
        self.slots = {(0, 0): 0, (1, 0): 0}
        self.order = []
        for level in self.levels:
            for at in level:
                for way in range(2):
                    if at <= self.reach[way]:
                        self.slots[way, at] = len(self.order) + 1
                        self.order.append((way, at))
        self.lengths = sorted({child - at for child, at in self.parent.items()})

    def children(self, way, at):
        return [child for child in TREE.get(at, ()) if child <= self.reach[way]]


def kernel(
    zlo_size,
    scale_ref,
    bias_ref,
    image_hbm,
    text_hbm,
    grad_image_ref,
    grad_text_ref,
    image_raw,
    text_raw,
    images,
    texts,
    dlogits,
    partial,
    back_out,
    back_in,
    core_out,
    core_in,
    held,
    outer_out,
    outer_in,
    inner_out,
    inner_in,
    half_sum,
    half_out,
    half_in,
    load_sems,
    token_sems,
    send_sems,
    recv_sems,
):
    rows, width = text_raw.shape
    blocks = zlo_size
    spread = Spread(blocks)
    side = RING * CORES * RING * rows
    z_size = zlo_size * HALVES

    loss = lax.axis_index("loss")
    y = lax.axis_index("section")
    mp = lax.axis_index("mp")
    z_lo = lax.div(loss, RING)
    x = lax.rem(loss, RING)
    z_half = lax.div(mp, CORES)
    core = lax.rem(mp, CORES)
    z = z_half * zlo_size + z_lo

    def device(x_steps=0, y_steps=0, z_steps=0, core_steps=0):
        z_at = lax.rem(z + (z_steps + z_size), z_size)
        return {
            "loss": lax.rem(z_at, zlo_size) * RING + lax.rem(x + (x_steps + RING), RING),
            "section": lax.rem(y + (y_steps + RING), RING),
            "mp": lax.div(z_at, zlo_size) * CORES + lax.rem(core + core_steps, CORES),
        }

    z_far = device(z_steps=zlo_size)
    x_next, x_prev, x_far = device(x_steps=1), device(x_steps=-1), device(x_steps=2)
    y_next, y_prev, y_far = device(y_steps=1), device(y_steps=-1), device(y_steps=2)
    sibling = device(core_steps=1)
    along_z = {steps: device(z_steps=steps) for length in spread.lengths for steps in (length, -length)}
    neighbours = [*along_z.values(), x_next, x_prev, x_far, y_next, y_prev, y_far, sibling]

    barrier = pltpu.get_barrier_semaphore()
    for neighbour in neighbours:
        pl.semaphore_signal(barrier, inc=1, device_id=neighbour, device_id_type=MESH)

    load_text = pltpu.make_async_copy(text_hbm, text_raw, load_sems.at[0])
    load_image = pltpu.make_async_copy(image_hbm, image_raw, load_sems.at[1])
    load_text.start()
    load_image.start()

    plan = Plan(send_sems, recv_sems)
    load_text.wait()
    texts[0] = unit_rows(text_raw[...])[0].astype(BF16)

    def normalize(core_steps):
        for half_at in range(HALVES):
            for y_steps in range(RING):
                y_at = lax.rem(y + y_steps, RING)
                half = z_half if half_at == 1 else 1 - z_half
                core_at = lax.rem(core + core_steps, CORES)
                start = pl.multiple_of(((y_at * HALVES + half) * CORES + core_at) * rows, rows)
                low = unit_rows(image_raw[pl.ds(start, rows), :])[0].astype(BF16)
                images[X_OWN, half_at, core_steps, y_steps] = low

    pl.semaphore_wait(barrier, len(neighbours))

    def pass_on(way, at):
        for child in spread.children(way, at):
            target = along_z[child - at if way == 0 else at - child]
            source, slot = spread.slots[way, at], spread.slots[way, child]
            plan.send(("t", way, child), texts.at[source], texts.at[slot], target)

    def text_level(level):
        for at in spread.levels[level]:
            for way in range(2):
                if at <= spread.reach[way]:
                    near = spread.lengths[0] * (1 - 2 * way)
                    plan.arrive(("t", way, at), texts.at[spread.slots[way, at]], along_z[near])
                    pass_on(way, at)

    pass_on(0, 0)
    pass_on(1, 0)
    load_image.wait()
    normalize(0)

    for half_at in range(HALVES):
        own = images.at[X_OWN, half_at, 0]
        plan.send(("xn", half_at), own, images.at[X_PREV, half_at, 0], x_next)
        other = 1 - half_at
        own = images.at[X_OWN, other, 0]
        plan.send(("xp", other), own, images.at[X_NEXT, other, 0], x_prev)

    normalize(1)

    def to_sibling(x_at, half_at):
        mine, theirs = images.at[x_at, half_at, 0], images.at[x_at, half_at, 1]
        plan.send(("xc", x_at, half_at), mine, theirs, sibling)

    def image_near(half_at):
        other = 1 - half_at
        from_prev, from_next = images.at[X_PREV, half_at, 0], images.at[X_NEXT, other, 0]
        plan.arrive(("xn", half_at), from_prev, x_next)
        if half_at == 0:
            plan.send(("xf", 0), from_prev, images.at[X_FAR, 0, 0], x_next)
        plan.arrive(("xp", other), from_next, x_prev)
        if half_at == 0:
            plan.send(("xf", 1), from_next, images.at[X_FAR, 1, 0], x_prev)
        to_sibling(X_PREV, half_at)
        to_sibling(X_NEXT, other)

    def image_far():
        for half_at in range(HALVES):
            plan.arrive(("xf", half_at), images.at[X_FAR, half_at, 0], x_next)
            to_sibling(X_FAR, half_at)

    def from_sibling(*x_ats):
        for half_at in range(HALVES):
            for x_at in x_ats:
                plan.arrive(("xc", x_at, half_at), images.at[x_at, half_at, 1], sibling)

    scale = scale_ref[0, 0]
    bias = bias_ref[0, 0]
    per_x = HALVES * CORES * RING * rows
    per_half = CORES * RING * rows

    def batch(slots, first, last):
        count = (last - first) * per_x
        low_row, high_row = slots[0] * rows, slots[1] * rows
        block = texts[slots[0] : slots[1]].reshape(high_row - low_row, width)
        every = images[first:last].reshape(count, width)
        logits = scale * lax.dot_general(
            block, every, (((1,), (1,)), ((), ())), preferred_element_type=F32
        )
        slope = jax.nn.sigmoid(logits + bias)
        if first == X_OWN and slots[0] == 0:
            text_ids = lax.broadcasted_iota(jnp.int32, slope.shape, 0)
            image_ids = lax.broadcasted_iota(jnp.int32, slope.shape, 1)
            positive = (text_ids < rows) & (image_ids == text_ids + per_half)
            slope = slope - jnp.where(positive, 1.0, 0.0)
        low = slope.astype(BF16)
        for x_at in range(first, last):
            for half_at in range(HALVES):
                start = (x_at - first) * per_x + half_at * per_half
                part = low[:, start : start + per_half]
                dlogits[half_at, low_row:high_row, x_at * per_half : (x_at + 1) * per_half] = part
        grads = jnp.dot(low, every, preferred_element_type=F32).reshape(-1, rows, width)
        if first == X_OWN:
            partial[slots[0] : slots[1]] = grads
        else:
            partial[slots[0] : slots[1]] += grads

    def back(level):
        for at in spread.levels[level]:
            for way in range(2):
                if at <= spread.reach[way]:
                    slot = spread.slots[way, at]
                    total = partial[slot]
                    for child in spread.children(way, at):
                        total = total + back_arrival(way, child)
                    back_out[slot] = total.astype(BF16)
                    length = at - spread.parent[at]
                    target = along_z[length if way == 1 else -length]
                    plan.send(("b", way, at), back_out.at[slot], back_in.at[slot], target)

    def back_arrival(way, child):
        slot = spread.slots[way, child]
        near = spread.lengths[0] * (2 * way - 1)
        plan.arrive(("b", way, child), back_in.at[slot], along_z[near])
        return back_in[slot].astype(F32)

    def image_partial(half_at):
        every = texts[...].reshape(blocks * rows, width)
        total = lax.dot_general(
            dlogits[half_at], every, (((0,), (0,)), ((), ())), preferred_element_type=F32
        )
        total = total.reshape(RING, CORES, RING, rows, width)
        core_out[half_at] = total[:, 1].astype(BF16)
        plan.send(("c", half_at), core_out.at[half_at], core_in.at[half_at], sibling)
        held[half_at] = total[:, 0]

    split = (width // 128 + 1) // 2 * 128
    columns = (slice(0, split), slice(split, width))
    x_targets = ((X_FAR, x_far), (X_NEXT, x_next), (X_PREV, x_prev))
    y_targets = ((Y_FAR, y_far), (Y_NEXT, y_next), (Y_PREV, y_prev))
    outer_targets, inner_targets = (x_targets, y_targets), (y_targets, x_targets)

    def at_block(half_at, part, outer):
        if part == 0:
            return (half_at, outer, slice(None), slice(None), columns[0])
        return (half_at, slice(None), outer, slice(None), columns[1])

    def at_line(half_at, part, *at):
        return (half_at, *at, slice(None), slice(None), columns[part])

    def summed(index):
        return held[index] + core_in[index].astype(F32)

    def outer_start(half_at):
        plan.arrive(("c", half_at), core_in.at[half_at], sibling)
        for way in range(RING - 1):
            for part in range(2):
                at, to = outer_targets[part][way]
                index = at_block(half_at, part, at)
                outer_out[index] = summed(index).astype(BF16)
                plan.send(("o", half_at, part, at), outer_out.at[index], outer_in.at[at_line(half_at, part, at)], to)

    def inner_start(half_at):
        for part in range(2):
            total = summed(at_block(half_at, part, 0))
            for at, to in reversed(outer_targets[part]):
                line = at_line(half_at, part, at)
                plan.arrive(("o", half_at, part, at), outer_in.at[line], to)
                total = total + outer_in[line].astype(F32)
            inner_out[at_line(half_at, part)] = total.astype(BF16)
            for at, to in inner_targets[part]:
                block = (half_at, at, slice(None), columns[part])
                plan.send(("i", half_at, part, at), inner_out.at[block], inner_in.at[block], to)
            half_sum[half_at, :, columns[part]] = total[0]

    def inner_end(half_at, part):
        total = half_sum[half_at, :, columns[part]]
        for at, to in reversed(inner_targets[part]):
            block = (half_at, at, slice(None), columns[part])
            plan.arrive(("i", half_at, part, at), inner_in.at[block], to)
            total = total + inner_in[block].astype(F32)
        if half_at == 0:
            half_out[:, columns[part]] = total.astype(BF16)
        else:
            half_sum[half_at, :, columns[part]] = total

    def give_token(at):
        pl.semaphore_signal(token_sems.at[at], inc=1, device_id=token_target, device_id_type=MESH)

    def take_token(at):
        pl.semaphore_wait(token_sems.at[at], 1)

    token_target = along_z[spread.lengths[-1]]
    last = len(spread.levels) - 1
    cut = min(spread.slots[way, at] for way, at in spread.order if at in spread.levels[last])
    early, late = (0, cut), (cut, blocks)
    for level in range(last):
        text_level(level)
        if level < HALVES:
            image_near(level)
    for level in range(last, HALVES):
        image_near(level)
    image_far()
    from_sibling(X_PREV, X_NEXT)
    batch(early, X_OWN, X_FAR)
    text_level(last)
    give_token(0)
    from_sibling(X_FAR)
    batch(late, X_OWN, X_FAR + 1)
    back(last)
    batch(early, X_FAR, X_FAR + 1)

    image_partial(0)
    image_partial(1)
    take_token(0)
    give_token(1)
    outer_start(0)
    for level in range(last - 1, 0, -1):
        back(level)
    inner_start(0)
    if last > 0:
        back(0)
    inner_end(0, 0)
    inner_end(0, 1)
    take_token(1)
    plan.send(("h",), half_out, half_in, z_far)
    outer_start(1)

    total = partial[0]
    for way in range(2):
        for child in spread.children(way, 0):
            total = total + back_arrival(way, child)
    unit_text, text_scaling = unit_rows(text_raw[...])
    grad_text_ref[...] = unit_backward(unit_text, text_scaling, scale * total)

    inner_start(1)
    inner_end(1, 0)
    inner_end(1, 1)
    own_row = pl.multiple_of(((y * HALVES + z_half) * CORES + core) * rows, rows)
    unit_image, image_scaling = unit_rows(image_raw[pl.ds(own_row, rows), :])
    plan.arrive(("h",), half_in, z_far)
    total = half_sum[1] + half_in[...].astype(F32)
    grad_image_ref[...] = unit_backward(unit_image, image_scaling, scale * total)
    plan.finish()


def per_device(image_embed, text_embed, logit_scale, logit_bias):
    rows, width = text_embed.shape
    zlo_size = lax.axis_size("loss") // RING
    blocks = zlo_size

    def scratch(*shape, dtype=BF16):
        return pltpu.VMEM((*shape, rows, width), dtype)

    smem = pl.BlockSpec(memory_space=pltpu.SMEM)
    vmem = pl.BlockSpec(memory_space=pltpu.VMEM)
    anywhere = pl.BlockSpec(memory_space=pl.ANY)
    return pl.pallas_call(
        functools.partial(kernel, zlo_size),
        out_shape=[jax.ShapeDtypeStruct((rows, width), F32)] * 2,
        in_specs=[smem, smem, anywhere, anywhere],
        out_specs=[vmem, vmem],
        scratch_shapes=[
            pltpu.VMEM(image_embed.shape, BF16),
            pltpu.VMEM(text_embed.shape, BF16),
            scratch(RING, HALVES, CORES, RING),
            scratch(blocks),
            pltpu.VMEM((HALVES, blocks * rows, RING * CORES * RING * rows), BF16),
            scratch(blocks, dtype=F32),
            scratch(blocks),
            scratch(blocks),
            scratch(HALVES, RING, RING),
            scratch(HALVES, RING, RING),
            scratch(HALVES, RING, RING, dtype=F32),
            scratch(HALVES, RING, RING),
            scratch(HALVES, RING, RING),
            scratch(HALVES, RING),
            scratch(HALVES, RING),
            scratch(HALVES, dtype=F32),
            scratch(),
            scratch(),
            pltpu.SemaphoreType.DMA((2,)),
            pltpu.SemaphoreType.REGULAR((2,)),
            pltpu.SemaphoreType.DMA((MOST_COPIES,)),
            pltpu.SemaphoreType.DMA((MOST_COPIES,)),
        ],
        compiler_params=pltpu.CompilerParams(
            collective_id=0, has_side_effects=True, vmem_limit_bytes=60 * 1024 * 1024
        ),
    )(logit_scale.reshape(1, 1), logit_bias.reshape(1, 1), image_embed, text_embed)


def solution(mesh):
    placed = (P("loss", None), P(("loss", "section", "mp"), None), P(), P())
    return jax.shard_map(
        per_device,
        mesh=mesh,
        in_specs=placed,
        out_specs=(P(("loss", "section", "mp"), None), P(("loss", "section", "mp"), None)),
        check_vma=False,
    )
```

```python
import functools

import jax
import jax.numpy as jnp
from jax import lax
from jax.experimental import pallas as pl
from jax.experimental.pallas import tpu as pltpu
from jax.sharding import PartitionSpec as P

epsilon = 1e-06
MESH = pl.DeviceIdType.MESH
F32 = jnp.float32
BF16 = jnp.bfloat16

RING = 4
HALVES = 2
CORES = 2
MOST_COPIES = 112

TREE = {0: (3, 1), 3: (6, 4), 1: (2,), 6: (8, 7), 4: (5,)}

X_OWN, X_PREV, X_NEXT, X_FAR = range(4)
Y_OWN, Y_NEXT, Y_FAR, Y_PREV = range(4)


def unit_rows(values):
    widened = values.astype(F32)
    scaling = lax.rsqrt(jnp.sum(widened * widened, axis=-1, keepdims=True) + epsilon)
    return (widened * scaling, scaling)


def unit_backward(unit, scaling, gradient):
    return (gradient - unit * jnp.sum(unit * gradient, axis=-1, keepdims=True)) * scaling


class Plan:
    def __init__(self, send_sems, recv_sems):
        self.send_sems = send_sems
        self.recv_sems = recv_sems
        self.numbers = {}
        self.sends = []

    def copy(self, key, source, target, device):
        at = self.numbers.setdefault(key, len(self.numbers))
        return pltpu.make_async_remote_copy(
            src_ref=source,
            dst_ref=target,
            send_sem=self.send_sems.at[at],
            recv_sem=self.recv_sems.at[at],
            device_id=device,
            device_id_type=MESH,
        )

    def send(self, key, source, target, device):
        copy = self.copy(key, source, target, device)
        copy.start()
        self.sends.append(copy)

    def arrive(self, key, target, device):
        self.copy(key, target, target, device).wait_recv()

    def finish(self):
        for copy in self.sends:
            copy.wait_send()


class Spread:
    def __init__(self, blocks):
        self.reach = (blocks // 2, blocks - 1 - blocks // 2)
        self.parent = {}
        self.levels = []
        level = [0]
        while level:
            found = []
            for at in level:
                for child in TREE.get(at, ()):
                    if child <= max(self.reach):
                        self.parent[child] = at
                        found.append(child)
            level = found
            if found:
                self.levels.append(found)
        self.slots = {(0, 0): 0, (1, 0): 0}
        self.order = []
        for level in self.levels:
            for at in level:
                for way in range(2):
                    if at <= self.reach[way]:
                        self.slots[way, at] = len(self.order) + 1
                        self.order.append((way, at))
        self.lengths = sorted({child - at for child, at in self.parent.items()})

    def children(self, way, at):
        return [child for child in TREE.get(at, ()) if child <= self.reach[way]]


def kernel(
    zlo_size,
    scale_ref,
    bias_ref,
    image_hbm,
    text_hbm,
    grad_image_ref,
    grad_text_ref,
    image_raw,
    text_raw,
    images,
    texts,
    dlogits,
    partial,
    back_out,
    back_in,
    core_out,
    core_in,
    held,
    outer_out,
    outer_in,
    inner_out,
    inner_in,
    half_sum,
    half_out,
    half_in,
    load_sems,
    token_sems,
    send_sems,
    recv_sems,
):
    rows, width = text_raw.shape
    blocks = zlo_size
    spread = Spread(blocks)
    side = RING * CORES * RING * rows
    z_size = zlo_size * HALVES

    loss = lax.axis_index("loss")
    y = lax.axis_index("section")
    mp = lax.axis_index("mp")
    z_lo = lax.div(loss, RING)
    x = lax.rem(loss, RING)
    z_half = lax.div(mp, CORES)
    core = lax.rem(mp, CORES)
    z = z_half * zlo_size + z_lo

    def device(x_steps=0, y_steps=0, z_steps=0, core_steps=0):
        z_at = lax.rem(z + (z_steps + z_size), z_size)
        return {
            "loss": lax.rem(z_at, zlo_size) * RING + lax.rem(x + (x_steps + RING), RING),
            "section": lax.rem(y + (y_steps + RING), RING),
            "mp": lax.div(z_at, zlo_size) * CORES + lax.rem(core + core_steps, CORES),
        }

    z_far = device(z_steps=zlo_size)
    x_next, x_prev, x_far = device(x_steps=1), device(x_steps=-1), device(x_steps=2)
    y_next, y_prev, y_far = device(y_steps=1), device(y_steps=-1), device(y_steps=2)
    sibling = device(core_steps=1)
    along_z = {steps: device(z_steps=steps) for length in spread.lengths for steps in (length, -length)}
    neighbours = [*along_z.values(), x_next, x_prev, x_far, y_next, y_prev, y_far, sibling]

    barrier = pltpu.get_barrier_semaphore()
    for neighbour in neighbours:
        pl.semaphore_signal(barrier, inc=1, device_id=neighbour, device_id_type=MESH)

    load_text = pltpu.make_async_copy(text_hbm, text_raw, load_sems.at[0])
    load_image = pltpu.make_async_copy(image_hbm, image_raw, load_sems.at[1])
    load_text.start()
    load_image.start()

    plan = Plan(send_sems, recv_sems)
    load_text.wait()
    texts[0] = unit_rows(text_raw[...])[0].astype(BF16)

    def normalize(core_steps):
        for half_at in range(HALVES):
            for y_steps in range(RING):
                y_at = lax.rem(y + y_steps, RING)
                half = z_half if half_at == 1 else 1 - z_half
                core_at = lax.rem(core + core_steps, CORES)
                start = pl.multiple_of(((y_at * HALVES + half) * CORES + core_at) * rows, rows)
                low = unit_rows(image_raw[pl.ds(start, rows), :])[0].astype(BF16)
                images[X_OWN, half_at, core_steps, y_steps] = low

    pl.semaphore_wait(barrier, len(neighbours))

    def pass_on(way, at):
        for child in spread.children(way, at):
            target = along_z[child - at if way == 0 else at - child]
            source, slot = spread.slots[way, at], spread.slots[way, child]
            plan.send(("t", way, child), texts.at[source], texts.at[slot], target)

    def text_level(level):
        for at in spread.levels[level]:
            for way in range(2):
                if at <= spread.reach[way]:
                    near = spread.lengths[0] * (1 - 2 * way)
                    plan.arrive(("t", way, at), texts.at[spread.slots[way, at]], along_z[near])
                    pass_on(way, at)

    pass_on(0, 0)
    pass_on(1, 0)
    load_image.wait()
    normalize(0)

    for half_at in range(HALVES):
        own = images.at[X_OWN, half_at, 0]
        plan.send(("xn", half_at), own, images.at[X_PREV, half_at, 0], x_next)
        other = 1 - half_at
        own = images.at[X_OWN, other, 0]
        plan.send(("xp", other), own, images.at[X_NEXT, other, 0], x_prev)

    normalize(1)

    def to_sibling(x_at, half_at):
        mine, theirs = images.at[x_at, half_at, 0], images.at[x_at, half_at, 1]
        plan.send(("xc", x_at, half_at), mine, theirs, sibling)

    def image_near(half_at):
        other = 1 - half_at
        from_prev, from_next = images.at[X_PREV, half_at, 0], images.at[X_NEXT, other, 0]
        plan.arrive(("xn", half_at), from_prev, x_next)
        if half_at == 0:
            plan.send(("xf", 0), from_prev, images.at[X_FAR, 0, 0], x_next)
        plan.arrive(("xp", other), from_next, x_prev)
        if half_at == 0:
            plan.send(("xf", 1), from_next, images.at[X_FAR, 1, 0], x_prev)
        to_sibling(X_PREV, half_at)
        to_sibling(X_NEXT, other)

    def image_far():
        for half_at in range(HALVES):
            plan.arrive(("xf", half_at), images.at[X_FAR, half_at, 0], x_next)
            to_sibling(X_FAR, half_at)

    def from_sibling(*x_ats):
        for half_at in range(HALVES):
            for x_at in x_ats:
                plan.arrive(("xc", x_at, half_at), images.at[x_at, half_at, 1], sibling)

    scale = scale_ref[0, 0]
    bias = bias_ref[0, 0]
    per_x = HALVES * CORES * RING * rows
    per_half = CORES * RING * rows

    def batch(slots, first, last):
        count = (last - first) * per_x
        low_row, high_row = slots[0] * rows, slots[1] * rows
        block = texts[slots[0] : slots[1]].reshape(high_row - low_row, width)
        every = images[first:last].reshape(count, width)
        logits = scale * lax.dot_general(
            block, every, (((1,), (1,)), ((), ())), preferred_element_type=F32
        )
        slope = jax.nn.sigmoid(logits + bias)
        if first == X_OWN and slots[0] == 0:
            text_ids = lax.broadcasted_iota(jnp.int32, slope.shape, 0)
            image_ids = lax.broadcasted_iota(jnp.int32, slope.shape, 1)
            positive = (text_ids < rows) & (image_ids == text_ids + per_half)
            slope = slope - jnp.where(positive, 1.0, 0.0)
        low = slope.astype(BF16)
        for x_at in range(first, last):
            for half_at in range(HALVES):
                start = (x_at - first) * per_x + half_at * per_half
                part = low[:, start : start + per_half]
                dlogits[half_at, low_row:high_row, x_at * per_half : (x_at + 1) * per_half] = part
        grads = jnp.dot(low, every, preferred_element_type=F32).reshape(-1, rows, width)
        if first == X_OWN:
            partial[slots[0] : slots[1]] = grads
        else:
            partial[slots[0] : slots[1]] += grads

    def back(level):
        for at in spread.levels[level]:
            for way in range(2):
                if at <= spread.reach[way]:
                    slot = spread.slots[way, at]
                    total = partial[slot]
                    for child in spread.children(way, at):
                        total = total + back_arrival(way, child)
                    back_out[slot] = total.astype(BF16)
                    length = at - spread.parent[at]
                    target = along_z[length if way == 1 else -length]
                    plan.send(("b", way, at), back_out.at[slot], back_in.at[slot], target)

    def back_arrival(way, child):
        slot = spread.slots[way, child]
        near = spread.lengths[0] * (2 * way - 1)
        plan.arrive(("b", way, child), back_in.at[slot], along_z[near])
        return back_in[slot].astype(F32)

    def image_partial(half_at):
        every = texts[...].reshape(blocks * rows, width)
        total = lax.dot_general(
            dlogits[half_at], every, (((0,), (0,)), ((), ())), preferred_element_type=F32
        )
        total = total.reshape(RING, CORES, RING, rows, width)
        core_out[half_at] = total[:, 1].astype(BF16)
        plan.send(("c", half_at), core_out.at[half_at], core_in.at[half_at], sibling)
        held[half_at] = total[:, 0]

    split = (width // 128 + 1) // 2 * 128
    columns = (slice(0, split), slice(split, width))
    x_targets = ((X_FAR, x_far), (X_NEXT, x_next), (X_PREV, x_prev))
    y_targets = ((Y_FAR, y_far), (Y_NEXT, y_next), (Y_PREV, y_prev))
    outer_targets, inner_targets = (x_targets, y_targets), (y_targets, x_targets)

    def at_block(half_at, part, outer):
        if part == 0:
            return (half_at, outer, slice(None), slice(None), columns[0])
        return (half_at, slice(None), outer, slice(None), columns[1])

    def at_line(half_at, part, *at):
        return (half_at, *at, slice(None), slice(None), columns[part])

    def summed(index):
        return held[index] + core_in[index].astype(F32)

    def outer_start(half_at):
        plan.arrive(("c", half_at), core_in.at[half_at], sibling)
        for way in range(RING - 1):
            for part in range(2):
                at, to = outer_targets[part][way]
                index = at_block(half_at, part, at)
                outer_out[index] = summed(index).astype(BF16)
                plan.send(("o", half_at, part, at), outer_out.at[index], outer_in.at[at_line(half_at, part, at)], to)

    def inner_start(half_at):
        for part in range(2):
            total = summed(at_block(half_at, part, 0))
            for at, to in reversed(outer_targets[part]):
                line = at_line(half_at, part, at)
                plan.arrive(("o", half_at, part, at), outer_in.at[line], to)
                total = total + outer_in[line].astype(F32)
            inner_out[at_line(half_at, part)] = total.astype(BF16)
            for at, to in inner_targets[part]:
                block = (half_at, at, slice(None), columns[part])
                plan.send(("i", half_at, part, at), inner_out.at[block], inner_in.at[block], to)
            half_sum[half_at, :, columns[part]] = total[0]

    def inner_end(half_at, part):
        total = half_sum[half_at, :, columns[part]]
        for at, to in reversed(inner_targets[part]):
            block = (half_at, at, slice(None), columns[part])
            plan.arrive(("i", half_at, part, at), inner_in.at[block], to)
            total = total + inner_in[block].astype(F32)
        if half_at == 0:
            half_out[:, columns[part]] = total.astype(BF16)
        else:
            half_sum[half_at, :, columns[part]] = total

    def give_token(at):
        pl.semaphore_signal(token_sems.at[at], inc=1, device_id=token_target, device_id_type=MESH)

    def take_token(at):
        pl.semaphore_wait(token_sems.at[at], 1)

    token_target = along_z[spread.lengths[-1]]
    last = len(spread.levels) - 1
    cut = min(spread.slots[way, at] for way, at in spread.order if at in spread.levels[last])
    early, late = (0, cut), (cut, blocks)
    for level in range(last):
        text_level(level)
        if level < HALVES:
            image_near(level)
    for level in range(last, HALVES):
        image_near(level)
    image_far()
    from_sibling(X_PREV, X_NEXT)
    batch(early, X_OWN, X_FAR)
    text_level(last)
    give_token(0)
    from_sibling(X_FAR)
    batch(late, X_OWN, X_FAR + 1)
    back(last)
    batch(early, X_FAR, X_FAR + 1)

    image_partial(0)
    image_partial(1)
    outer_start(0)
    take_token(0)
    give_token(1)
    for level in range(last - 1, 0, -1):
        back(level)
    inner_start(0)
    if last > 0:
        back(0)
    inner_end(0, 0)
    inner_end(0, 1)
    take_token(1)
    plan.send(("h",), half_out, half_in, z_far)
    outer_start(1)

    inner_start(1)
    total = partial[0]
    for way in range(2):
        for child in spread.children(way, 0):
            total = total + back_arrival(way, child)
    unit_text, text_scaling = unit_rows(text_raw[...])
    grad_text_ref[...] = unit_backward(unit_text, text_scaling, scale * total)

    inner_end(1, 0)
    inner_end(1, 1)
    own_row = pl.multiple_of(((y * HALVES + z_half) * CORES + core) * rows, rows)
    unit_image, image_scaling = unit_rows(image_raw[pl.ds(own_row, rows), :])
    plan.arrive(("h",), half_in, z_far)
    total = half_sum[1] + half_in[...].astype(F32)
    grad_image_ref[...] = unit_backward(unit_image, image_scaling, scale * total)
    plan.finish()


def per_device(image_embed, text_embed, logit_scale, logit_bias):
    rows, width = text_embed.shape
    zlo_size = lax.axis_size("loss") // RING
    blocks = zlo_size

    def scratch(*shape, dtype=BF16):
        return pltpu.VMEM((*shape, rows, width), dtype)

    smem = pl.BlockSpec(memory_space=pltpu.SMEM)
    vmem = pl.BlockSpec(memory_space=pltpu.VMEM)
    anywhere = pl.BlockSpec(memory_space=pl.ANY)
    return pl.pallas_call(
        functools.partial(kernel, zlo_size),
        out_shape=[jax.ShapeDtypeStruct((rows, width), F32)] * 2,
        in_specs=[smem, smem, anywhere, anywhere],
        out_specs=[vmem, vmem],
        scratch_shapes=[
            pltpu.VMEM(image_embed.shape, BF16),
            pltpu.VMEM(text_embed.shape, BF16),
            scratch(RING, HALVES, CORES, RING),
            scratch(blocks),
            pltpu.VMEM((HALVES, blocks * rows, RING * CORES * RING * rows), BF16),
            scratch(blocks, dtype=F32),
            scratch(blocks),
            scratch(blocks),
            scratch(HALVES, RING, RING),
            scratch(HALVES, RING, RING),
            scratch(HALVES, RING, RING, dtype=F32),
            scratch(HALVES, RING, RING),
            scratch(HALVES, RING, RING),
            scratch(HALVES, RING),
            scratch(HALVES, RING),
            scratch(HALVES, dtype=F32),
            scratch(),
            scratch(),
            pltpu.SemaphoreType.DMA((2,)),
            pltpu.SemaphoreType.REGULAR((2,)),
            pltpu.SemaphoreType.DMA((MOST_COPIES,)),
            pltpu.SemaphoreType.DMA((MOST_COPIES,)),
        ],
        compiler_params=pltpu.CompilerParams(
            collective_id=0, has_side_effects=True, vmem_limit_bytes=60 * 1024 * 1024
        ),
    )(logit_scale.reshape(1, 1), logit_bias.reshape(1, 1), image_embed, text_embed)


def solution(mesh):
    placed = (P("loss", None), P(("loss", "section", "mp"), None), P(), P())
    return jax.shard_map(
        per_device,
        mesh=mesh,
        in_specs=placed,
        out_specs=(P(("loss", "section", "mp"), None), P(("loss", "section", "mp"), None)),
        check_vma=False,
    )
```
